32 devices in a mesh: rep: 2 (over y), ep: 16 (over z, x, core).
Axes of the slice: x: 2, y: 2, z: 4, core: 2. Of those that a mesh axis runs over, the one named last changes fastest.
Arguments:
- tokens: bfloat16 [256, 3072], P(('rep', 'ep')), parts along dimension 0, may hold values from -6 to 6
- expert_ids: int32 [256, 2], P(('rep', 'ep')), parts along dimension 0, may hold values from 0 to 7, all different within a row; in each aligned block of 8 rows (0 to 7, 8 to 15, ...) at most 4 rows name the same one
- gate_fixed: int32 [256, 2], P(('rep', 'ep')), parts along dimension 0, may hold values from 256 to 4096
- w_gate: bfloat16 [3072, 65536], P(None, 'ep'), may hold values from -0.109375 to 0.109375
- w_up: bfloat16 [3072, 65536], P(None, 'ep'), may hold values from -0.109375 to 0.109375
- w_down: bfloat16 [65536, 3072], P('ep'), may hold values from -0.0625 to 0.0625
Outputs:
- mixed: bfloat16 [256, 3072], P(('rep', 'ep')), parts along dimension 0
The draws below stay inside these ranges and needn't reach their ends.
There are 2 independent parts, one for each index of `rep`. The reference program is written for one: setup_inputs(seed, part) draws one part's arguments, and reference() takes and returns one part's arrays. A program takes and returns all parts, laid end to end along the dimension named above; an argument that names none is the same for every part. Nothing has to cross between parts.
Inputs may be any that keep to these rules, and one draw needn't show every extreme that they name: `expert_ids`: each token names two different experts; among the 8 tokens of one device no expert is named more than 4 times, and in every draw some device names some expert exactly 4 times.
All inputs are finite; a program needn't handle non-finite values.
Results may differ from the reference program's by a relative error of at most 0.0057.
Values may be sent and summed in bfloat16 or wider, within the bound.
A program may use at most 128 MiB of HBM per device.

```python
import math
import jax
import jax.numpy as jnp
import numpy as np
from jax import lax

D = 3072
FF = 8192
EXPERTS = 8
TOK_DEV = 8
SLOT = 4
TOKENS = 128
N_EP = 16


def plant(values, stream_key, smallest, largest):
    shape = values.shape
    index_at = [jax.random.randint(jax.random.fold_in(stream_key, axis), (), 0, shape[axis]) for axis in range(len(shape))]
    values = values.at[tuple(index_at)].set(smallest)
    longest = shape.index(max(shape))
    index_at[longest] = (index_at[longest] + 1) % shape[longest]
    return values.at[tuple(index_at)].set(largest)


def shard_levels(own_key, shape, shards, smallest, high):
    gain, own = 1.0, jax.random.fold_in(own_key, 6)
    for dim, parts in shards:
        heights = jnp.exp(jax.random.uniform(jax.random.fold_in(own, dim), (parts,), jnp.float32, smallest / len(shards), high / len(shards)))
        gain = gain * jnp.repeat(heights, shape[dim] // parts).reshape([-1 if axis == dim else 1 for axis in range(len(shape))])
    return gain


def routed_block(key, own, number, rows, number_of, top, bound, skew):
    sequence = jax.random.permutation(key, number_of)
    heavy_load, common = portions_of(number_of, rows * top, bound, skew, True), portions_of(number_of, rows * top, bound, skew, False)
    places = jnp.arange(number_of)

    def named(tallies, offset_by):
        used = int((tallies > 0).sum())
        fixed = max(1, used // 4)
        passed = fixed + (places - fixed + offset_by * (used - fixed)) % max(1, number_of - fixed)
        return jnp.zeros((number_of,), jnp.int32).at[sequence[jnp.where(places < fixed, places, passed)]].set(jnp.asarray(tallies, jnp.int32))

    tallies = jnp.where(number % 4 == 0, named(heavy_load, number // 4), named(common, number - number // 4 - 1))
    mixed = jax.random.permutation(jax.random.fold_in(own, 3), number_of)
    giver, taker = mixed[0:number_of // 2 * 2:2], mixed[1:number_of // 2 * 2:2]
    margin = jnp.minimum(tallies[giver] - 1, bound - tallies[taker]) // 2
    margin = jnp.where((giver == sequence[0]) | (taker == sequence[0]) | (tallies[taker] == 0), 0, jnp.maximum(margin, 0))
    passed = jax.random.randint(jax.random.fold_in(own, 4), (number_of // 2,), 0, 1 << 20) % (margin + 1)
    tallies = tallies.at[giver].add(-passed).at[taker].add(passed)
    items = jnp.searchsorted(jnp.cumsum(tallies), jnp.arange(rows * top), side="right").astype(jnp.int32)
    listing = items.reshape(top, rows).T
    listing = listing[jax.random.permutation(jax.random.fold_in(own, 1), rows)]
    offset_by = jax.random.randint(jax.random.fold_in(own, 2), (rows, 1), 0, top)
    return jnp.take_along_axis(listing, (jnp.arange(top)[None, :] + offset_by) % top, axis=1)


def portions_of(amount, total, limit, skew, full):
    loads = [(1 << 20) // math.isqrt(grade ** skew) + 1 for grade in range(1, amount + 1)]
    largest = limit if full else min(limit, max(-(-total // amount), total * loads[0] // sum(loads)))
    least = 1 if total - largest >= amount - 1 else 0
    holding, spare = [largest] + [least] * (amount - 1), total - largest - least * (amount - 1)
    while spare > 0:
        candidates = [i for i in range(1, amount) if holding[i] < largest] or [i for i in range(1, amount) if holding[i] < limit]
        whole, left = sum([loads[i] for i in candidates]), spare
        for i in candidates:
            more = min(limit - holding[i], max(1, left * loads[i] // whole), spare)
            holding[i] = holding[i] + more
            spare = spare - more
    return np.array(holding)


def bell_draw(key, shape, width, reach, cuts=(), kind=jnp.bfloat16):
    factor_of = shard_levels(key, shape, cuts, -0.22, 0.18) if cuts else 1.0
    values = jax.random.normal(key, shape, jnp.float32) * width * factor_of
    return jnp.minimum(jnp.maximum(values, -reach), reach).astype(kind)


def setup_inputs(seed: int = 0, part: int = 0) -> dict:
    key_of = jax.random.split(jax.random.key(seed), 7)
    part_splits = jax.random.split(jax.random.fold_in(key_of[6], part), 7)
    tokens = bell_draw(part_splits[0], (TOKENS, D), 1.0, 6.0, ((0, 16),))
    expert_ids_keys = jax.random.split(jax.random.fold_in(part_splits[1], 1), TOKENS // TOK_DEV)
    expert_ids_turns = jax.random.permutation(jax.random.fold_in(part_splits[1], 3), TOKENS // TOK_DEV)
    expert_ids = jax.vmap(lambda own, number: routed_block(jax.random.fold_in(part_splits[1], 2), own, number, TOK_DEV, EXPERTS, 2, SLOT, 2))(expert_ids_keys, expert_ids_turns).reshape((TOKENS, 2))
    gate_fixed = plant(jax.random.randint(part_splits[2], (TOKENS, 2), 256, 4097), jax.random.fold_in(part_splits[2], 1), 256, 4096).astype(jnp.int32)
    w_gate = bell_draw(key_of[3], (D, EXPERTS * FF), D ** -0.5, 0.109375, ((1, 16),))
    w_up = bell_draw(key_of[4], (D, EXPERTS * FF), D ** -0.5, 0.109375, ((1, 16),))
    w_down = bell_draw(key_of[5], (EXPERTS * FF, D), FF ** -0.5, 0.0625, ((0, 16),))
    return dict(tokens=tokens, expert_ids=expert_ids, gate_fixed=gate_fixed, w_gate=w_gate, w_up=w_up, w_down=w_down)


def reference(tokens, expert_ids, gate_fixed, w_gate, w_up, w_down):
    group_size = N_EP // EXPERTS
    hid_width = FF // group_size
    capacity = SLOT * N_EP
    gate_values = gate_fixed.astype(jnp.float32) / 4096.0
    result = jnp.zeros((TOKENS, D), jnp.float32)
    for expert in range(EXPERTS):
        chosen = expert_ids == expert
        routed = jnp.any(chosen, axis=1)
        expert_weight = jnp.sum(jnp.where(chosen, gate_values, 0.0), axis=1)
        ordering = jnp.cumsum(routed.astype(jnp.int32)) - 1
        target = jnp.where(routed, ordering, capacity).astype(jnp.int32)
        source = jnp.zeros((capacity,), jnp.int32).at[target].set(jnp.arange(TOKENS, dtype=jnp.int32), mode="drop")
        present = jnp.zeros((capacity,), jnp.bool_).at[target].set(True, mode="drop")
        row_block = jnp.where(present[:, None], tokens[source], jnp.zeros((), tokens.dtype))
        start = expert * FF
        gate_part = jnp.dot(row_block, w_gate[:, start:start + FF], preferred_element_type=jnp.float32)
        up_part = jnp.dot(row_block, w_up[:, start:start + FF], preferred_element_type=jnp.float32)
        hidden = (jax.nn.silu(gate_part) * up_part).astype(jnp.bfloat16)
        down_slices = w_down[start:start + FF].reshape(group_size, hid_width, D)
        hidden_slices = jnp.swapaxes(hidden.reshape(capacity, group_size, hid_width), 0, 1)

        def add_slice(running, pieces):
            partial_value = jnp.dot(pieces[0], pieces[1], preferred_element_type=jnp.float32).astype(jnp.bfloat16)
            return running + partial_value.astype(jnp.float32), None

        summed, _ = lax.scan(add_slice, jnp.zeros((capacity, D), jnp.float32), (hidden_slices, down_slices))
        picked = summed[jnp.clip(ordering, 0, capacity - 1).astype(jnp.int32)]
        result = result + jnp.where(routed[:, None], expert_weight[:, None] * picked, 0.0)
    return result.astype(jnp.bfloat16)
```

```python
import functools

import jax
import jax.numpy as jnp
from jax import lax
from jax.experimental import pallas as pl
from jax.experimental.pallas import tpu as pltpu
from jax.sharding import PartitionSpec as P

EXPERTS = 8
SLOT = 4
QUARTERS = 4
PIECE = SLOT * QUARTERS
F_CHUNK = 256
N_CHUNK = 512
MAX_SLOTS = 8
MESH = pl.DeviceIdType.MESH
F32 = jnp.float32
BF16 = jnp.bfloat16


def iota(shape, dim):
    return lax.broadcasted_iota(jnp.int32, shape, dim)


def kernel(
    n_ep, f_chunk, n_chunk, slots,
    tok_ref, ids_ref, gate_ref, wg_ref, wu_ref, wd_ref, out_ref,
    wbuf, dbuf, send_buf, recv_buf, x_ref, hidden, pack, pair_recv, sum_buf, comb,
    w_sem, d_sem, a_send, a_recv, b_send, b_recv, c_send, c_recv, e_send, e_recv,
):
    n_chip = n_ep // 2
    chips_per_expert = n_chip // EXPERTS
    rep = lax.axis_index("rep")
    me = lax.axis_index("ep")
    core = lax.rem(me, 2)
    chip = me // 2
    partner = me + 1 - 2 * core
    width = tok_ref.shape[1]
    quarter = width // QUARTERS
    n_f = wg_ref.shape[1] // f_chunk
    n_n = width // n_chunk
    sub = n_chunk // QUARTERS
    n_tok = tok_ref.shape[0]
    rows = n_ep * SLOT

    def w_copies(f, slot):
        cols = pl.ds(pl.multiple_of(f * f_chunk, f_chunk), f_chunk)
        return (
            pltpu.make_async_copy(wg_ref.at[:, cols], wbuf.at[slot, 0], w_sem.at[slot, 0]),
            pltpu.make_async_copy(wu_ref.at[:, cols], wbuf.at[slot, 1], w_sem.at[slot, 1]),
        )

    def d_copy(n):
        cols = pl.ds(pl.multiple_of(n * n_chunk, n_chunk), n_chunk)
        return pltpu.make_async_copy(wd_ref.at[:, cols], dbuf.at[n], d_sem.at[n])

    barrier = pltpu.get_barrier_semaphore()

    def greet(i, _):
        to = lax.rem(chip + i, n_chip) * 2 + core
        pl.semaphore_signal(barrier, inc=1, device_id=(rep, to), device_id_type=MESH)
        return 0

    lax.fori_loop(1, n_chip, greet, 0)
    pl.semaphore_signal(barrier, inc=1, device_id=(rep, partner), device_id_type=MESH)

    def first(f, _):
        for copy in w_copies(f, f):
            copy.start()
        return 0

    lax.fori_loop(0, slots, first, 0)

    ids0 = ids_ref[:, 0:1]
    ids1 = ids_ref[:, 1:2]
    below = (iota((n_tok, n_tok), 1) < iota((n_tok, n_tok), 0)).astype(F32)

    def ranks(lanes, per_expert):
        lane = iota((n_tok, lanes), 1)
        expert = lane // (PIECE * per_expert)
        hit0, hit1 = ids0 == expert, ids1 == expert
        count = jnp.dot(below, (hit0 | hit1).astype(F32), preferred_element_type=F32)
        fits = count.astype(jnp.int32) == lax.rem(lane, SLOT)
        place = lax.rem(lane // SLOT, QUARTERS)
        return hit0 & fits, hit1 & fits, place

    hit0, hit1, place = ranks(EXPERTS * PIECE, 1)
    hit = hit0 | hit1
    piece = jnp.zeros((EXPERTS * PIECE, quarter), F32)
    for q in range(QUARTERS):
        mask = (hit & (place == q)).astype(F32).T.astype(BF16)
        piece += jnp.dot(
            mask, tok_ref[:, q * quarter:(q + 1) * quarter], preferred_element_type=F32
        )
    send_buf[...] = piece.astype(BF16)

    pl.semaphore_wait(barrier, n_chip)

    def rows_at(k):
        return pl.ds(pl.multiple_of(k * PIECE, PIECE), PIECE)

    def a_copy(to, source):
        return pltpu.make_async_remote_copy(
            src_ref=send_buf.at[rows_at(to // chips_per_expert)],
            dst_ref=recv_buf.at[rows_at(source * 2 + core)],
            send_sem=a_send.at[to],
            recv_sem=a_recv.at[source],
            device_id=(rep, to * 2 + core),
            device_id_type=MESH,
        )

    def b_copy(source, side):
        return pltpu.make_async_remote_copy(
            src_ref=recv_buf.at[rows_at(source * 2 + side)],
            dst_ref=recv_buf.at[rows_at(source * 2 + side)],
            send_sem=b_send.at[source],
            recv_sem=b_recv.at[source],
            device_id=(rep, partner),
            device_id_type=MESH,
        )

    def send_a(i, _):
        a_copy(lax.rem(chip + i, n_chip), chip).start()
        return 0

    lax.fori_loop(1, n_chip, send_a, 0)
    recv_buf[rows_at(me)] = send_buf[rows_at(chip // chips_per_expert)]
    b_copy(chip, core).start()

    def early(n, _):
        d_copy(n).start()
        return 0

    lax.fori_loop(0, n_n, early, 0)

    def forward(i, _):
        source = lax.rem(chip + n_chip - i, n_chip)
        a_copy(source, source).wait_recv()
        b_copy(source, core).start()
        return 0

    lax.fori_loop(1, n_chip, forward, 0)

    def arrived(i, _):
        b_copy(i, 1 - core).wait_recv()
        return 0

    lax.fori_loop(0, n_chip, arrived, 0)

    r = iota((rows, n_ep * PIECE), 0)
    l = iota((rows, n_ep * PIECE), 1)
    at = (r // SLOT) * PIECE + lax.rem(r, SLOT)
    for q in range(QUARTERS):
        take = (l == at + q * SLOT).astype(BF16)
        x_ref[:, q * quarter:(q + 1) * quarter] = jnp.dot(
            take, recv_buf[...], preferred_element_type=F32
        ).astype(BF16)

    def up_step(f, _):
        slot = lax.rem(f, slots)
        for copy in w_copies(f, slot):
            copy.wait()
        gate_part = jnp.dot(x_ref[...], wbuf[slot, 0], preferred_element_type=F32)
        up_part = jnp.dot(x_ref[...], wbuf[slot, 1], preferred_element_type=F32)
        value = gate_part / (1.0 + jnp.exp(-gate_part)) * up_part
        hidden[:, pl.ds(pl.multiple_of(f * f_chunk, f_chunk), f_chunk)] = value.astype(BF16)

        @pl.when(f + slots < n_f)
        def _():
            for copy in w_copies(f + slots, slot):
                copy.start()

        return 0

    lax.fori_loop(0, n_f, up_step, 0)

    half = n_chip * PIECE
    pr = iota((2 * half, rows), 0)
    side = lax.rem(pr // half + core, 2)
    owner = lax.rem(pr, half) // PIECE
    wanted = (owner * 2 + side) * SLOT + lax.rem(pr, SLOT)
    pack_hit = iota((2 * half, rows), 1) == wanted
    pack_place = lax.rem(pr // SLOT, QUARTERS)
    pack_q = [(pack_hit & (pack_place == q)).astype(BF16) for q in range(QUARTERS)]

    def c_copy(n):
        return pltpu.make_async_remote_copy(
            src_ref=pack.at[n, 1],
            dst_ref=pair_recv.at[n],
            send_sem=c_send.at[n],
            recv_sem=c_recv.at[n],
            device_id=(rep, partner),
            device_id_type=MESH,
        )

    def e_copy(n, to, source):
        return pltpu.make_async_remote_copy(
            src_ref=sum_buf.at[n, rows_at(to)],
            dst_ref=comb.at[n, rows_at(source)],
            send_sem=e_send.at[n, to],
            recv_sem=e_recv.at[n, source],
            device_id=(rep, to * 2 + core),
            device_id_type=MESH,
        )

    def down(n):
        d_copy(n).wait()
        part = jnp.dot(hidden[...], dbuf[n], preferred_element_type=F32).astype(BF16)
        packed = jnp.zeros((2 * half, sub), F32)
        for q in range(QUARTERS):
            packed += jnp.dot(
                pack_q[q], part[:, q * sub:(q + 1) * sub], preferred_element_type=F32
            )
        packed = packed.astype(BF16)
        pack[n, 0] = packed[:half]
        pack[n, 1] = packed[half:]
        c_copy(n).start()

    def reduce_send(n):
        c_copy(n).wait_recv()
        total = pack[n, 0].astype(F32) + pair_recv[n].astype(F32)
        sum_buf[n] = total.astype(BF16)

        def send_e(i, _):
            e_copy(n, lax.rem(chip + i, n_chip), chip).start()
            return 0

        lax.fori_loop(1, n_chip, send_e, 0)
        comb[n, rows_at(chip)] = sum_buf[n, rows_at(chip)]

    down(0)

    def down_step(n, _):
        down(n)
        reduce_send(n - 1)
        return 0

    lax.fori_loop(1, n_n, down_step, 0)
    reduce_send(n_n - 1)

    hit0, hit1, place = ranks(half, chips_per_expert)
    picks = jnp.concatenate(
        [(h & (place == q)).astype(F32) for h in (hit0, hit1) for q in range(QUARTERS)], axis=0
    ).astype(BF16)
    weights = gate_ref[...].astype(F32) / 4096.0
    g0, g1 = weights[:, 0:1], weights[:, 1:2]

    for n in range(n_n):

        def come(i, _):
            source = lax.rem(chip + n_chip - i, n_chip)
            e_copy(n, source, source).wait_recv()
            return 0

        lax.fori_loop(1, n_chip, come, 0)
        picked = jnp.dot(picks, comb[n], preferred_element_type=F32)
        for q in range(QUARTERS):
            k0 = picked[q * n_tok:(q + 1) * n_tok]
            k1 = picked[(QUARTERS + q) * n_tok:(QUARTERS + q + 1) * n_tok]
            start = n * n_chunk + q * sub
            out_ref[:, start:start + sub] = (g0 * k0 + g1 * k1).astype(BF16)

    def drain(i, _):
        to = lax.rem(chip + i, n_chip)
        a_copy(to, chip).wait_send()
        b_copy(to, core).wait_send()
        for n in range(n_n):
            e_copy(n, to, chip).wait_send()
        return 0

    lax.fori_loop(1, n_chip, drain, 0)
    b_copy(chip, core).wait_send()
    for n in range(n_n):
        c_copy(n).wait_send()


def shards(tokens, expert_ids, gate_fixed, w_gate, w_up, w_down):
    n_ep = lax.axis_size("ep")
    n_chip = n_ep // 2
    n_tok, width = tokens.shape
    ff = w_gate.shape[1]
    f_chunk = min(F_CHUNK, ff)
    n_chunk = min(N_CHUNK, width)
    n_f, n_n = ff // f_chunk, width // n_chunk
    slots = min(MAX_SLOTS, n_f)
    rows = n_ep * SLOT
    half = n_chip * PIECE
    sub = n_chunk // QUARTERS
    dma = pltpu.SemaphoreType.DMA
    vmem = pl.BlockSpec(memory_space=pltpu.VMEM)
    hbm = pl.BlockSpec(memory_space=pl.ANY)
    return pl.pallas_call(
        functools.partial(kernel, n_ep, f_chunk, n_chunk, slots),
        out_shape=jax.ShapeDtypeStruct((n_tok, width), BF16),
        in_specs=[vmem, vmem, vmem, hbm, hbm, hbm],
        out_specs=vmem,
        scratch_shapes=[
            pltpu.VMEM((slots, 2, width, f_chunk), BF16),
            pltpu.VMEM((n_n, ff, n_chunk), BF16),
            pltpu.VMEM((EXPERTS * PIECE, width // QUARTERS), BF16),
            pltpu.VMEM((n_ep * PIECE, width // QUARTERS), BF16),
            pltpu.VMEM((rows, width), BF16),
            pltpu.VMEM((rows, ff), BF16),
            pltpu.VMEM((n_n, 2, half, sub), BF16),
            pltpu.VMEM((n_n, half, sub), BF16),
            pltpu.VMEM((n_n, half, sub), BF16),
            pltpu.VMEM((n_n, half, sub), BF16),
            dma((slots, 2)),
            dma((n_n,)),
            dma((n_chip,)),
            dma((n_chip,)),
            dma((n_chip,)),
            dma((n_chip,)),
            dma((n_n,)),
            dma((n_n,)),
            dma((n_n, n_chip)),
            dma((n_n, n_chip)),
        ],
        compiler_params=pltpu.CompilerParams(
            collective_id=0, has_side_effects=True, vmem_limit_bytes=56 * 2**20
        ),
        cost_estimate=pl.CostEstimate(
            flops=6 * rows * width * ff, bytes_accessed=6 * width * ff, transcendentals=rows * ff
        ),
        name="moe",
    )(tokens, expert_ids, gate_fixed, w_gate, w_up, w_down)


def solution(mesh):
    in_specs = (
        P(("rep", "ep"), None),
        P(("rep", "ep"), None),
        P(("rep", "ep"), None),
        P(None, "ep"),
        P(None, "ep"),
        P("ep", None),
    )
    out_specs = P(("rep", "ep"), None)
    return jax.shard_map(shards, mesh=mesh, in_specs=in_specs, out_specs=out_specs, check_vma=False)
```

```python
import functools

import jax
import jax.numpy as jnp
from jax import lax
from jax.experimental import pallas as pl
from jax.experimental.pallas import tpu as pltpu
from jax.sharding import PartitionSpec as P

EXPERTS = 8
SLOT = 4
QUARTERS = 4
PIECE = SLOT * QUARTERS
F_CHUNK = 512
N_CHUNK = 1024
MAX_SLOTS = 4
EARLY = 1
MESH = pl.DeviceIdType.MESH
F32 = jnp.float32
BF16 = jnp.bfloat16


def iota(shape, dim):
    return lax.broadcasted_iota(jnp.int32, shape, dim)


def kernel(
    n_ep, f_chunk, n_chunk, slots,
    tok_ref, ids_ref, gate_ref, wg_ref, wu_ref, wd_ref, out_ref,
    wbuf, dbuf, send_buf, recv_buf, x_ref, hidden, pack, pair_recv, sum_buf, comb,
    w_sem, d_sem, a_send, a_recv, b_send, b_recv, c_send, c_recv, e_send, e_recv,
):
    n_chip = n_ep // 2
    chips_per_expert = n_chip // EXPERTS
    rep = lax.axis_index("rep")
    me = lax.axis_index("ep")
    core = lax.rem(me, 2)
    chip = me // 2
    partner = me + 1 - 2 * core
    width = tok_ref.shape[1]
    quarter = width // QUARTERS
    n_f = wg_ref.shape[1] // f_chunk
    n_n = width // n_chunk
    sub = n_chunk // QUARTERS
    n_tok = tok_ref.shape[0]
    early = min(EARLY, n_n)
    rows = n_ep * SLOT

    def w_copies(f, slot):
        cols = pl.ds(pl.multiple_of(f * f_chunk, f_chunk), f_chunk)
        return (
            pltpu.make_async_copy(wg_ref.at[:, cols], wbuf.at[slot, 0], w_sem.at[slot, 0]),
            pltpu.make_async_copy(wu_ref.at[:, cols], wbuf.at[slot, 1], w_sem.at[slot, 1]),
        )

    def d_copy(n):
        cols = pl.ds(pl.multiple_of(n * n_chunk, n_chunk), n_chunk)
        return pltpu.make_async_copy(wd_ref.at[:, cols], dbuf.at[n], d_sem.at[n])

    barrier = pltpu.get_barrier_semaphore()

    def greet(i, _):
        to = lax.rem(chip + i, n_chip) * 2 + core
        pl.semaphore_signal(barrier, inc=1, device_id=(rep, to), device_id_type=MESH)
        return 0

    lax.fori_loop(1, n_chip, greet, 0)
    pl.semaphore_signal(barrier, inc=1, device_id=(rep, partner), device_id_type=MESH)

    def first(f, _):
        for copy in w_copies(f, f):
            copy.start()
        return 0

    lax.fori_loop(0, slots, first, 0)

    own = iota((n_tok, n_tok), 0) == iota((n_tok, n_tok), 1)

    def column(row):
        return jnp.sum(jnp.where(own, row.astype(F32), 0.0), axis=1, keepdims=True)

    ids0 = column(ids_ref[0:1]).astype(jnp.int32)
    ids1 = column(ids_ref[1:2]).astype(jnp.int32)
    below = (iota((n_tok, n_tok), 1) < iota((n_tok, n_tok), 0)).astype(F32)

    def ranks(lanes, per_expert):
        lane = iota((n_tok, lanes), 1)
        expert = lane // (PIECE * per_expert)
        hit0, hit1 = ids0 == expert, ids1 == expert
        count = jnp.dot(below, (hit0 | hit1).astype(F32), preferred_element_type=F32)
        fits = count.astype(jnp.int32) == lax.rem(lane, SLOT)
        place = lax.rem(lane // SLOT, QUARTERS)
        return hit0 & fits, hit1 & fits, place

    hit0, hit1, place = ranks(EXPERTS * PIECE, 1)
    hit = hit0 | hit1
    piece = jnp.zeros((EXPERTS * PIECE, quarter), F32)
    for q in range(QUARTERS):
        mask = (hit & (place == q)).astype(F32).T.astype(BF16)
        piece += jnp.dot(
            mask, tok_ref[:, q * quarter:(q + 1) * quarter], preferred_element_type=F32
        )
    send_buf[...] = piece.astype(BF16)

    pl.semaphore_wait(barrier, n_chip)

    def rows_at(k):
        return pl.ds(pl.multiple_of(k * PIECE, PIECE), PIECE)

    def a_copy(to, source):
        return pltpu.make_async_remote_copy(
            src_ref=send_buf.at[rows_at(to // chips_per_expert)],
            dst_ref=recv_buf.at[rows_at(source * 2 + core)],
            send_sem=a_send.at[to],
            recv_sem=a_recv.at[source],
            device_id=(rep, to * 2 + core),
            device_id_type=MESH,
        )

    def b_copy(source, side):
        return pltpu.make_async_remote_copy(
            src_ref=recv_buf.at[rows_at(source * 2 + side)],
            dst_ref=recv_buf.at[rows_at(source * 2 + side)],
            send_sem=b_send.at[source],
            recv_sem=b_recv.at[source],
            device_id=(rep, partner),
            device_id_type=MESH,
        )

    def send_a(i, _):
        a_copy(lax.rem(chip + i, n_chip), chip).start()
        return 0

    lax.fori_loop(1, n_chip, send_a, 0)
    recv_buf[rows_at(me)] = send_buf[rows_at(chip // chips_per_expert)]
    b_copy(chip, core).start()

    for n in range(early):
        d_copy(n).start()

    def forward(i, _):
        source = lax.rem(chip + n_chip - i, n_chip)
        a_copy(source, source).wait_recv()
        b_copy(source, core).start()
        return 0

    lax.fori_loop(1, n_chip, forward, 0)

    def arrived(i, _):
        b_copy(i, 1 - core).wait_recv()
        return 0

    lax.fori_loop(0, n_chip, arrived, 0)

    r = iota((rows, n_ep * PIECE), 0)
    l = iota((rows, n_ep * PIECE), 1)
    at = (r // SLOT) * PIECE + lax.rem(r, SLOT)
    for q in range(QUARTERS):
        take = (l == at + q * SLOT).astype(BF16)
        x_ref[:, q * quarter:(q + 1) * quarter] = jnp.dot(
            take, recv_buf[...], preferred_element_type=F32
        ).astype(BF16)

    def up_step(f, _):
        slot = lax.rem(f, slots)
        for copy in w_copies(f, slot):
            copy.wait()
        gate_part = jnp.dot(x_ref[...], wbuf[slot, 0], preferred_element_type=F32)
        up_part = jnp.dot(x_ref[...], wbuf[slot, 1], preferred_element_type=F32)
        value = gate_part / (1.0 + jnp.exp(-gate_part)) * up_part
        hidden[:, pl.ds(pl.multiple_of(f * f_chunk, f_chunk), f_chunk)] = value.astype(BF16)

        @pl.when(f + slots < n_f)
        def _():
            for copy in w_copies(f + slots, slot):
                copy.start()

        @pl.when(f == max(n_f - slots - 1, 0))
        def _():
            for n in range(early, n_n):
                d_copy(n).start()

        return 0

    lax.fori_loop(0, n_f, up_step, 0)

    half = n_chip * PIECE
    pr = iota((2 * half, rows), 0)
    side = lax.rem(pr // half + core, 2)
    owner = lax.rem(pr, half) // PIECE
    wanted = (owner * 2 + side) * SLOT + lax.rem(pr, SLOT)
    pack_hit = iota((2 * half, rows), 1) == wanted
    pack_place = lax.rem(pr // SLOT, QUARTERS)
    pack_q = [(pack_hit & (pack_place == q)).astype(BF16) for q in range(QUARTERS)]

    def c_copy(n):
        return pltpu.make_async_remote_copy(
            src_ref=pack.at[n, 1],
            dst_ref=pair_recv.at[n],
            send_sem=c_send.at[n],
            recv_sem=c_recv.at[n],
            device_id=(rep, partner),
            device_id_type=MESH,
        )

    def e_copy(n, to, source):
        return pltpu.make_async_remote_copy(
            src_ref=sum_buf.at[n, rows_at(to)],
            dst_ref=comb.at[n, rows_at(source)],
            send_sem=e_send.at[n, to],
            recv_sem=e_recv.at[n, source],
            device_id=(rep, to * 2 + core),
            device_id_type=MESH,
        )

    def down(n):
        d_copy(n).wait()
        part = jnp.dot(hidden[...], dbuf[n], preferred_element_type=F32).astype(BF16)
        packed = jnp.zeros((2 * half, sub), F32)
        for q in range(QUARTERS):
            packed += jnp.dot(
                pack_q[q], part[:, q * sub:(q + 1) * sub], preferred_element_type=F32
            )
        packed = packed.astype(BF16)
        pack[n, 0] = packed[:half]
        pack[n, 1] = packed[half:]
        c_copy(n).start()

    def reduce_send(n):
        c_copy(n).wait_recv()
        total = pack[n, 0].astype(F32) + pair_recv[n].astype(F32)
        sum_buf[n] = total.astype(BF16)

        def send_e(i, _):
            e_copy(n, lax.rem(chip + i, n_chip), chip).start()
            return 0

        lax.fori_loop(1, n_chip, send_e, 0)
        comb[n, rows_at(chip)] = sum_buf[n, rows_at(chip)]

    down(0)

    def down_step(n, _):
        down(n)
        reduce_send(n - 1)
        return 0

    lax.fori_loop(1, n_n, down_step, 0)
    reduce_send(n_n - 1)

    hit0, hit1, place = ranks(half, chips_per_expert)
    picks = jnp.concatenate(
        [(h & (place == q)).astype(F32) for h in (hit0, hit1) for q in range(QUARTERS)], axis=0
    ).astype(BF16)
    g0, g1 = column(gate_ref[0:1]) / 4096.0, column(gate_ref[1:2]) / 4096.0

    for n in range(n_n):

        def come(i, _):
            source = lax.rem(chip + n_chip - i, n_chip)
            e_copy(n, source, source).wait_recv()
            return 0

        lax.fori_loop(1, n_chip, come, 0)
        picked = jnp.dot(picks, comb[n], preferred_element_type=F32)
        for q in range(QUARTERS):
            k0 = picked[q * n_tok:(q + 1) * n_tok]
            k1 = picked[(QUARTERS + q) * n_tok:(QUARTERS + q + 1) * n_tok]
            start = n * n_chunk + q * sub
            out_ref[:, start:start + sub] = (g0 * k0 + g1 * k1).astype(BF16)

    def drain(i, _):
        to = lax.rem(chip + i, n_chip)
        a_copy(to, chip).wait_send()
        b_copy(to, core).wait_send()
        for n in range(n_n):
            e_copy(n, to, chip).wait_send()
        return 0

    lax.fori_loop(1, n_chip, drain, 0)
    b_copy(chip, core).wait_send()
    for n in range(n_n):
        c_copy(n).wait_send()


def shards(tokens, expert_ids, gate_fixed, w_gate, w_up, w_down):
    n_ep = lax.axis_size("ep")
    n_chip = n_ep // 2
    n_tok, width = tokens.shape
    ff = w_gate.shape[1]
    f_chunk = min(F_CHUNK, ff)
    n_chunk = min(N_CHUNK, width)
    n_f, n_n = ff // f_chunk, width // n_chunk
    slots = min(MAX_SLOTS, n_f)
    rows = n_ep * SLOT
    half = n_chip * PIECE
    sub = n_chunk // QUARTERS
    dma = pltpu.SemaphoreType.DMA
    vmem = pl.BlockSpec(memory_space=pltpu.VMEM)
    hbm = pl.BlockSpec(memory_space=pl.ANY)
    return pl.pallas_call(
        functools.partial(kernel, n_ep, f_chunk, n_chunk, slots),
        out_shape=jax.ShapeDtypeStruct((n_tok, width), BF16),
        in_specs=[vmem, vmem, vmem, hbm, hbm, hbm],
        out_specs=vmem,
        scratch_shapes=[
            pltpu.VMEM((slots, 2, width, f_chunk), BF16),
            pltpu.VMEM((n_n, ff, n_chunk), BF16),
            pltpu.VMEM((EXPERTS * PIECE, width // QUARTERS), BF16),
            pltpu.VMEM((n_ep * PIECE, width // QUARTERS), BF16),
            pltpu.VMEM((rows, width), BF16),
            pltpu.VMEM((rows, ff), BF16),
            pltpu.VMEM((n_n, 2, half, sub), BF16),
            pltpu.VMEM((n_n, half, sub), BF16),
            pltpu.VMEM((n_n, half, sub), BF16),
            pltpu.VMEM((n_n, half, sub), BF16),
            dma((slots, 2)),
            dma((n_n,)),
            dma((n_chip,)),
            dma((n_chip,)),
            dma((n_chip,)),
            dma((n_chip,)),
            dma((n_n,)),
            dma((n_n,)),
            dma((n_n, n_chip)),
            dma((n_n, n_chip)),
        ],
        compiler_params=pltpu.CompilerParams(
            collective_id=0, has_side_effects=True, vmem_limit_bytes=56 * 2**20
        ),
        cost_estimate=pl.CostEstimate(
            flops=6 * rows * width * ff, bytes_accessed=6 * width * ff, transcendentals=rows * ff
        ),
        name="moe",
    )(tokens, expert_ids.T, gate_fixed.T, w_gate, w_up, w_down)


def solution(mesh):
    in_specs = (
        P(("rep", "ep"), None),
        P(("rep", "ep"), None),
        P(("rep", "ep"), None),
        P(None, "ep"),
        P(None, "ep"),
        P("ep", None),
    )
    out_specs = P(("rep", "ep"), None)
    return jax.shard_map(shards, mesh=mesh, in_specs=in_specs, out_specs=out_specs, check_vma=False)
```
